32 devices in a mesh: samples: 2 (over y), grid: 16 (over z, x, core).
Axes of the slice: x: 2, y: 2, z: 4, core: 2. Of those that a mesh axis runs over, the one named last changes fastest.
Arguments:
- hamiltonian: float32 [64, 4, 128, 128], P('grid'), may hold values from -0.25 to 0.25
- columns: int32 [64, 4], P('grid'), may hold values from 0 to 63, as said below
- sample: int32 [2], P('samples'), parts along dimension 0, may hold values from 0 to 1023
Outputs:
- density: float32 [128, 4, 128, 128], P(('samples', 'grid')), parts along dimension 0
The draws below stay inside these ranges and needn't reach their ends.
There are 2 independent parts, one for each index of `samples`. The reference program is written for one: setup_inputs(seed, part) draws one part's arguments, and reference() takes and returns one part's arrays. A program takes and returns all parts, laid end to end along the dimension named above; an argument that names none is the same for every part. Nothing has to cross between parts.
Inputs may be any that keep to these rules, and one draw needn't show every extreme that they name: `columns`: each row's entries are distinct and sorted, lie within cyclic distance 3 of the row's own index (modulo 64), and include the row's own index.
All inputs are finite; a program needn't handle non-finite values.
Results may differ from the reference program's by a relative error of at most 0.0003.
Values sent between devices are 32-bit elements; how exact they have to be, the bound alone decides.
A program may use at most 64 MiB of HBM per device.

```python
import jax
import jax.numpy as jnp
from jax import lax

TILE = 128
TILES_ROW = 4
REACH = 3
STEPS = 2
BLOCK_ROWS = 64


def draw_columns(key, part):
    key = jax.random.fold_in(key, 7)
    offsets = jnp.concatenate([jnp.arange(-REACH, 0, dtype=jnp.int32), jnp.arange(1, REACH + 1, dtype=jnp.int32)])
    row_keys = jax.random.split(key, BLOCK_ROWS)
    picked = jax.vmap(lambda k: jax.random.permutation(k, offsets)[:TILES_ROW - 1])(row_keys)
    picked = jnp.concatenate([jnp.zeros((BLOCK_ROWS, 1), jnp.int32), picked], axis=1)
    row_index = jnp.arange(BLOCK_ROWS, dtype=jnp.int32)[:, None]
    return jnp.sort(jnp.mod(row_index + picked, BLOCK_ROWS), axis=1).astype(jnp.int32)


def levels(stream_key, dims, cuts, least, largest):
    level, own = 1.0, jax.random.fold_in(stream_key, 6)
    for axis_at, blocks in cuts:
        draws = jnp.exp(jax.random.uniform(jax.random.fold_in(own, axis_at), (blocks,), jnp.float32, least / len(cuts), largest / len(cuts)))
        level = level * jnp.repeat(draws, dims[axis_at] // blocks).reshape([-1 if axis == axis_at else 1 for axis in range(len(dims))])
    return level


def gaussian(own_key, shape, spread, bound, shards=(), held_as=jnp.bfloat16):
    drawn = spread * jax.random.normal(own_key, shape, jnp.float32)
    if shards:
        drawn = drawn * levels(own_key, shape, shards, -0.22, 0.18)
    return jnp.clip(drawn, -bound, bound).astype(held_as)


def setup_inputs(seed: int = 0, part: int = 0) -> dict:
    arg_keys = jax.random.split(jax.random.key(seed), 4)
    part_keys = jax.random.split(jax.random.fold_in(arg_keys[3], part), 4)
    hamiltonian = gaussian(arg_keys[0], (BLOCK_ROWS, TILES_ROW, TILE, TILE), (TILES_ROW * TILE) ** -0.5, 0.25, ((0, 16),), jnp.float32)
    columns = draw_columns(jax.random.fold_in(arg_keys[3], 71), part)
    sample = jax.random.randint(part_keys[2], (1,), 0, 1024).astype(jnp.int32)
    return {"hamiltonian": hamiltonian, "columns": columns, "sample": sample}


def radical_of(sample):
    places = jnp.arange(10, dtype=jnp.int32)
    sample_bits = jnp.bitwise_and(jnp.right_shift(sample[0], places), 1).astype(jnp.float32)
    return jnp.sum(sample_bits * jnp.power(jnp.float32(0.5), (places + 1).astype(jnp.float32)))


def reference(hamiltonian, columns, sample):
    chemical = -0.2 + 0.4 * radical_of(sample)
    row_index = jnp.arange(BLOCK_ROWS, dtype=jnp.int32)[:, None]
    ondiag = (columns == row_index).astype(jnp.float32)[:, :, None, None]
    identity = jnp.eye(TILE, dtype=jnp.float32)
    density = 0.4 * (chemical * ondiag * identity - hamiltonian) + 0.5 * ondiag * identity

    for iteration in range(STEPS):
        def one_row(i):
            own_columns = columns[i]
            gathered = density[own_columns]
            remote_columns = columns[own_columns]
            matches = (remote_columns[:, :, None] == own_columns[None, None, :]).astype(jnp.float32)
            aligned = jnp.einsum("amb,amyz->abyz", matches, gathered, precision=lax.Precision.HIGHEST)
            square = jnp.einsum("axy,abyz->bxz", density[i], aligned, precision=lax.Precision.HIGHEST)
            cube = jnp.einsum("axy,abyz->bxz", square, aligned, precision=lax.Precision.HIGHEST)
            return 3.0 * square - 2.0 * cube

        density = lax.map(one_row, jnp.arange(BLOCK_ROWS, dtype=jnp.int32))
    return density
```

```python
import functools

import jax
import jax.numpy as jnp
from jax import lax
from jax.experimental import pallas as pl
from jax.experimental.pallas import tpu as pltpu
from jax.sharding import PartitionSpec as P

REACH = 3
STEPS = 2
ROWS = 4
HALO = STEPS * REACH
SPAN = ROWS + 2 * HALO
MESH = pl.DeviceIdType.MESH

ORDER = ((5, 0), (6, 0), (7, 0), (8, 0), (4, 0), (9, 0), (3, 0), (6, 1), (10, 0), (7, 1), (11, 0), (8, 1), (12, 0), (9, 1))


def pick(index, values):
    chosen = jnp.int32(values[0])
    for at, value in enumerate(values[1:], 1):
        chosen = jnp.where(index == at, jnp.int32(value), chosen)
    return chosen


def kernel(
    devices, ham, columns, sample, out, ext, cbuf, csm, high, low, eye, ahigh, alow, left, left2,
    recv, send, crecv, csend, local, csem,
):
    me, s = lax.axis_index("grid"), lax.axis_index("samples")
    slots, tile = ham.shape[1], ham.shape[2]
    pair = slots // 2
    total = devices * ROWS
    zero_tile = SPAN * slots
    odd = lax.rem(me, 2)
    sign = 2 * odd - 1

    def at(offset):
        return (s, lax.rem(me + offset + devices, devices))

    mate, outer, behind, beyond = at(-sign), at(sign), at(-2 * sign), at(2 * sign)
    peer = (1 - s, me)

    def own(u):
        return jnp.where(odd == 1, u - HALO, HALO + ROWS - 1 - u)

    def mine(u):
        return ext.at[u, pl.ds(pair * s, pair)]

    def theirs(u):
        return ext.at[u, pl.ds(pair * (1 - s), pair)]

    def copy(source, target, send_sem, recv_sem, device):
        return pltpu.make_async_remote_copy(
            src_ref=source, dst_ref=target, send_sem=send_sem, recv_sem=recv_sem, device_id=device, device_id_type=MESH
        )

    def to_mate(u):
        return copy(ham.at[own(u)], ext.at[11 - u], send.at[u - 6], recv.at[11 - u, 0], mate)

    def to_outer(u):
        return copy(ham.at[own(u), pl.ds(pair * s, pair)], mine(19 - u), send.at[4 + u - 6], recv.at[19 - u, s], outer)

    def to_behind(u):
        return copy(ham.at[own(u), pl.ds(pair * s, pair)], mine(u + 8), send.at[8 + u - 6], recv.at[u + 8, s], behind)

    def mine_to_peer(u):
        return copy(mine(u), mine(u), send.at[10 + u - 10], recv.at[u, s], peer)

    def mine_to_mate(u):
        return copy(mine(u), mine(11 - u), send.at[16 + u - 10], recv.at[11 - u, s], mate)

    def theirs_to_mate(u):
        return copy(theirs(u), theirs(11 - u), send.at[18 + u - 10], recv.at[11 - u, 1 - s], mate)

    def theirs_from_peer(u):
        return copy(theirs(u), theirs(u), send.at[10 + u - 10], recv.at[u, 1 - s], peer)

    def keep(u):
        return pltpu.make_async_copy(ham.at[own(u)], ext.at[u], local.at[u - 6])

    def columns_to(index):
        slot, device = ((1, mate), (3, outer), (4, behind), (0, beyond))[index]
        return copy(cbuf.at[2], cbuf.at[slot], csend.at[index], crecv.at[slot], device)

    barrier = pltpu.get_barrier_semaphore()
    for device in (mate, outer, behind, beyond, peer):
        pl.semaphore_signal(barrier, inc=1, device_id=device, device_id_type=MESH)
    for u in range(6, 10):
        keep(u).start()
    cbuf[2, 0:ROWS, 0:slots] = columns[...]
    pl.semaphore_wait(barrier, 5)

    for index in range(4):
        columns_to(index).start()
    for u in (9, 8, 7, 6):
        to_outer(u).start()
    for u in (6, 7):
        to_behind(u).start()
    for u in (6, 7, 8, 9):
        to_mate(u).start()

    same = lax.broadcasted_iota(jnp.int32, (tile, tile), 0) == lax.broadcasted_iota(jnp.int32, (tile, tile), 1)
    eye[...] = same.astype(jnp.float32)
    for step in range(STEPS):
        high[step, zero_tile] = jnp.zeros((tile, tile), jnp.bfloat16)
        low[step, zero_tile] = jnp.zeros((tile, tile), jnp.bfloat16)
    radical = jnp.float32(0.0)
    for bit in range(10):
        radical += (lax.shift_right_logical(sample[0], bit) & 1).astype(jnp.float32) * jnp.float32(0.5 ** (bit + 1))
    chemical = -0.2 + 0.4 * radical

    for index in range(4):
        columns_to(index).wait()
    table = pltpu.make_async_copy(cbuf, csm, csem)
    table.start()
    table.wait()

    def column(u, slot):
        place = (u + 2) & 3
        return csm[lax.shift_right_logical(u + 2, 2), jnp.where(odd == 1, place, 3 - place), slot]

    def row_of(col):
        up = jnp.clip(lax.rem(col - ROWS * me + HALO + total, total), 0, SPAN - 1)
        return jnp.where(odd == 1, up, SPAN - 1 - up)

    def split(value):
        upper = value.astype(jnp.bfloat16)
        return upper, (value - upper.astype(jnp.float32)).astype(jnp.bfloat16)

    def begin(u):
        for m in range(slots):
            diagonal = eye[...] * jnp.where(row_of(column(u, m)) == u, 1.0, 0.0)
            tiles = 0.4 * (chemical * diagonal - ext[u, m]) + 0.5 * diagonal
            upper, lower = split(tiles)
            high[0, u * slots + m] = upper
            low[0, u * slots + m] = lower

    def begin_each(first, last):
        def body(u, carry):
            begin(u)
            return carry

        lax.fori_loop(first, last, body, 0)

    def got(u):
        mine_to_peer(u).wait_recv()
        mine_to_peer(u).start()
        if u < 12:
            mine_to_mate(u).start()

    def got_rest(u):
        theirs_from_peer(u).wait_recv()
        if u < 12:
            theirs_to_mate(u).start()
        begin(u)

    def from_mate(u):
        mine_to_mate(11 - u).wait_recv()
        theirs_to_mate(11 - u).wait_recv()
        begin(u)

    def times(lefts):
        both = jnp.dot(lefts[...], ahigh[...], preferred_element_type=jnp.float32)
        rest = jnp.dot(lefts[0:tile], alow[...], preferred_element_type=jnp.float32)
        return both[0:tile] + (both[tile:] + rest)

    def work(u, step):
        own_columns = [column(u, b) for b in range(slots)]
        for a in range(slots):
            row = row_of(own_columns[a])
            held = [column(row, m) for m in range(slots)]
            for b in range(slots):
                index = jnp.int32(zero_tile)
                for m in range(slots):
                    index = jnp.where(held[m] == own_columns[b], row * slots + m, index)
                ahigh[a * tile : (a + 1) * tile, b * tile : (b + 1) * tile] = high[step, index]
                alow[a * tile : (a + 1) * tile, b * tile : (b + 1) * tile] = low[step, index]
        for m in range(slots):
            left[0:tile, m * tile : (m + 1) * tile] = high[step, u * slots + m]
            left[tile:, m * tile : (m + 1) * tile] = low[step, u * slots + m]
        square = times(left)
        upper, lower = split(square)
        left2[0:tile] = upper
        left2[tile:] = lower
        density = 3.0 * square - 2.0 * times(left2)

        @pl.when(step == 0)
        def _():
            upper, lower = split(density)
            for b in range(slots):
                high[1, u * slots + b] = upper[:, b * tile : (b + 1) * tile]
                low[1, u * slots + b] = lower[:, b * tile : (b + 1) * tile]

        @pl.when(step == 1)
        def _():
            for b in range(slots):
                out[own(u), b] = density[:, b * tile : (b + 1) * tile]

    for u in range(6, 10):
        keep(u).wait()
    for u in range(6, 10):
        to_mate(u).wait_recv()
    begin_each(2, 10)

    events = {
        2: lambda: (got(10), got(11), got_rest(10)),
        3: lambda: (got(12), got_rest(11)),
        4: lambda: (got(13), from_mate(1)),
        5: lambda: (got_rest(12),),
        6: lambda: (got(14), from_mate(0)),
        8: lambda: (got_rest(13),),
        10: lambda: (got(15), got_rest(14)),
        12: lambda: (got_rest(15),),
    }

    def body(turn, carry):
        for when, event in events.items():
            pl.when(turn == when)(lambda event=event: (event(), None)[1])
        work(pick(turn, [u for u, _ in ORDER]), pick(turn, [step for _, step in ORDER]))
        return carry

    lax.fori_loop(0, len(ORDER), body, 0)

    for u in (9, 8, 7, 6):
        to_outer(u).wait_send()
        to_mate(u).wait_send()
    for u in (6, 7):
        to_behind(u).wait_send()
    for u in range(10, 16):
        mine_to_peer(u).wait_send()
        if u < 12:
            mine_to_mate(u).wait_send()
            theirs_to_mate(u).wait_send()


def shards(hamiltonian, columns, sample):
    rows, slots, tile, _ = hamiltonian.shape
    devices = lax.axis_size("grid")
    assert rows == ROWS and devices >= 6
    dma = pltpu.SemaphoreType.DMA
    return pl.pallas_call(
        functools.partial(kernel, devices),
        out_shape=jax.ShapeDtypeStruct(hamiltonian.shape, jnp.float32),
        in_specs=[
            pl.BlockSpec(memory_space=pl.ANY),
            pl.BlockSpec(memory_space=pltpu.VMEM),
            pl.BlockSpec(memory_space=pltpu.SMEM),
        ],
        out_specs=pl.BlockSpec(memory_space=pltpu.VMEM),
        scratch_shapes=[
            pltpu.VMEM((SPAN, slots, tile, tile), jnp.float32),
            pltpu.VMEM((5, 8, 128), jnp.int32),
            pltpu.SMEM((5, 8, 128), jnp.int32),
            pltpu.VMEM((STEPS, SPAN * slots + 1, tile, tile), jnp.bfloat16),
            pltpu.VMEM((STEPS, SPAN * slots + 1, tile, tile), jnp.bfloat16),
            pltpu.VMEM((tile, tile), jnp.float32),
            pltpu.VMEM((slots * tile, slots * tile), jnp.bfloat16),
            pltpu.VMEM((slots * tile, slots * tile), jnp.bfloat16),
            pltpu.VMEM((2 * tile, slots * tile), jnp.bfloat16),
            pltpu.VMEM((2 * tile, slots * tile), jnp.bfloat16),
            dma((SPAN, 2)),
            dma((20,)),
            dma((5,)),
            dma((4,)),
            dma((4,)),
            dma,
        ],
        compiler_params=pltpu.CompilerParams(
            collective_id=0, has_side_effects=True, vmem_limit_bytes=40 * 2**20
        ),
    )(hamiltonian, columns, sample)


def solution(mesh):
    return jax.shard_map(
        shards,
        mesh=mesh,
        in_specs=(P("grid", None, None, None), P("grid", None), P("samples")),
        out_specs=P(("samples", "grid"), None, None, None),
        check_vma=False,
    )
```

```python
import functools

import jax
import jax.numpy as jnp
from jax import lax
from jax.experimental import pallas as pl
from jax.experimental.pallas import tpu as pltpu
from jax.sharding import PartitionSpec as P

REACH = 3
STEPS = 2
ROWS = 4
HALO = STEPS * REACH
SPAN = ROWS + 2 * HALO
MESH = pl.DeviceIdType.MESH

ORDER = ((5, 0), (6, 0), (7, 0), (4, 0), (8, 0), (3, 0), (9, 0), (6, 1), (10, 0), (7, 1), (11, 0), (8, 1), (12, 0), (9, 1))


def pick(index, values):
    chosen = jnp.int32(values[0])
    for at, value in enumerate(values[1:], 1):
        chosen = jnp.where(index == at, jnp.int32(value), chosen)
    return chosen


def kernel(
    devices, ham, columns, sample, out, ext, cbuf, csm, high, low, eye, ahigh, alow, left, left2,
    recv, send, crecv, csend, local, csem,
):
    me, s = lax.axis_index("grid"), lax.axis_index("samples")
    slots, tile = ham.shape[1], ham.shape[2]
    pair = slots // 2
    total = devices * ROWS
    zero_tile = SPAN * slots
    odd = lax.rem(me, 2)
    sign = 2 * odd - 1

    def at(offset):
        return (s, lax.rem(me + offset + devices, devices))

    mate, outer, behind, beyond = at(-sign), at(sign), at(-2 * sign), at(2 * sign)
    peer = (1 - s, me)

    def own(u):
        return jnp.where(odd == 1, u - HALO, HALO + ROWS - 1 - u)

    def mine(u):
        return ext.at[u, pl.ds(pair * s, pair)]

    def theirs(u):
        return ext.at[u, pl.ds(pair * (1 - s), pair)]

    def copy(source, target, send_sem, recv_sem, device):
        return pltpu.make_async_remote_copy(
            src_ref=source, dst_ref=target, send_sem=send_sem, recv_sem=recv_sem, device_id=device, device_id_type=MESH
        )

    def to_mate(u):
        return copy(ham.at[own(u)], ext.at[11 - u], send.at[u - 6], recv.at[11 - u, 0], mate)

    def to_outer(u):
        return copy(ham.at[own(u), pl.ds(pair * s, pair)], mine(19 - u), send.at[4 + u - 6], recv.at[19 - u, s], outer)

    def to_behind(u):
        return copy(ham.at[own(u), pl.ds(pair * s, pair)], mine(u + 8), send.at[8 + u - 6], recv.at[u + 8, s], behind)

    def mine_to_peer(u):
        return copy(mine(u), mine(u), send.at[10 + u - 10], recv.at[u, s], peer)

    def mine_to_mate(u):
        return copy(mine(u), mine(11 - u), send.at[16 + u - 10], recv.at[11 - u, s], mate)

    def theirs_to_mate(u):
        return copy(theirs(u), theirs(11 - u), send.at[18 + u - 10], recv.at[11 - u, 1 - s], mate)

    def theirs_from_peer(u):
        return copy(theirs(u), theirs(u), send.at[10 + u - 10], recv.at[u, 1 - s], peer)

    def keep(u):
        return pltpu.make_async_copy(ham.at[own(u)], ext.at[u], local.at[u - 6])

    def columns_to(index):
        slot, device = ((1, mate), (3, outer), (4, behind), (0, beyond))[index]
        return copy(cbuf.at[2], cbuf.at[slot], csend.at[index], crecv.at[slot], device)

    barrier = pltpu.get_barrier_semaphore()
    for device in (mate, outer, behind, beyond, peer):
        pl.semaphore_signal(barrier, inc=1, device_id=device, device_id_type=MESH)
    for u in range(6, 10):
        keep(u).start()
    cbuf[2, 0:ROWS, 0:slots] = columns[...]
    pl.semaphore_wait(barrier, 5)

    for index in range(4):
        columns_to(index).start()
    for u in (9, 8):
        to_outer(u).start()
    for u in (6, 7, 8, 9):
        to_mate(u).start()

    same = lax.broadcasted_iota(jnp.int32, (tile, tile), 0) == lax.broadcasted_iota(jnp.int32, (tile, tile), 1)
    eye[...] = same.astype(jnp.float32)
    for step in range(STEPS):
        high[step, zero_tile] = jnp.zeros((tile, tile), jnp.bfloat16)
        low[step, zero_tile] = jnp.zeros((tile, tile), jnp.bfloat16)
    radical = jnp.float32(0.0)
    for bit in range(10):
        radical += (lax.shift_right_logical(sample[0], bit) & 1).astype(jnp.float32) * jnp.float32(0.5 ** (bit + 1))
    chemical = -0.2 + 0.4 * radical

    for index in range(4):
        columns_to(index).wait()
    table = pltpu.make_async_copy(cbuf, csm, csem)
    table.start()
    table.wait()

    def column(u, slot):
        place = (u + 2) & 3
        return csm[lax.shift_right_logical(u + 2, 2), jnp.where(odd == 1, place, 3 - place), slot]

    def row_of(col):
        up = jnp.clip(lax.rem(col - ROWS * me + HALO + total, total), 0, SPAN - 1)
        return jnp.where(odd == 1, up, SPAN - 1 - up)

    def split(value):
        upper = value.astype(jnp.bfloat16)
        return upper, (value - upper.astype(jnp.float32)).astype(jnp.bfloat16)

    def begin(u):
        for m in range(slots):
            diagonal = eye[...] * jnp.where(row_of(column(u, m)) == u, 1.0, 0.0)
            tiles = 0.4 * (chemical * diagonal - ext[u, m]) + 0.5 * diagonal
            upper, lower = split(tiles)
            high[0, u * slots + m] = upper
            low[0, u * slots + m] = lower

    def begin_each(first, last):
        def body(u, carry):
            begin(u)
            return carry

        lax.fori_loop(first, last, body, 0)

    def got(u):
        mine_to_peer(u).wait_recv()
        mine_to_peer(u).start()
        if u < 12:
            mine_to_mate(u).start()
            to_outer(17 - u).start()
        elif u < 14:
            to_behind(u - 6).start()

    def got_rest(u):
        theirs_from_peer(u).wait_recv()
        if u < 12:
            theirs_to_mate(u).start()
        begin(u)

    def from_mate(u):
        mine_to_mate(11 - u).wait_recv()
        theirs_to_mate(11 - u).wait_recv()
        begin(u)

    def times(lefts):
        both = jnp.dot(lefts[...], ahigh[...], preferred_element_type=jnp.float32)
        rest = jnp.dot(lefts[0:tile], alow[...], preferred_element_type=jnp.float32)
        return both[0:tile] + (both[tile:] + rest)

    def work(u, step):
        own_columns = [column(u, b) for b in range(slots)]
        for a in range(slots):
            row = row_of(own_columns[a])
            held = [column(row, m) for m in range(slots)]
            for b in range(slots):
                index = jnp.int32(zero_tile)
                for m in range(slots):
                    index = jnp.where(held[m] == own_columns[b], row * slots + m, index)
                ahigh[a * tile : (a + 1) * tile, b * tile : (b + 1) * tile] = high[step, index]
                alow[a * tile : (a + 1) * tile, b * tile : (b + 1) * tile] = low[step, index]
        for m in range(slots):
            left[0:tile, m * tile : (m + 1) * tile] = high[step, u * slots + m]
            left[tile:, m * tile : (m + 1) * tile] = low[step, u * slots + m]
        square = times(left)
        upper, lower = split(square)
        left2[0:tile] = upper
        left2[tile:] = lower
        density = 3.0 * square - 2.0 * times(left2)

        @pl.when(step == 0)
        def _():
            upper, lower = split(density)
            for b in range(slots):
                high[1, u * slots + b] = upper[:, b * tile : (b + 1) * tile]
                low[1, u * slots + b] = lower[:, b * tile : (b + 1) * tile]

        @pl.when(step == 1)
        def _():
            for b in range(slots):
                out[own(u), b] = density[:, b * tile : (b + 1) * tile]

    for u in range(6, 10):
        keep(u).wait()
    for u in range(6, 10):
        to_mate(u).wait_recv()
    begin_each(2, 10)

    events = {
        0: lambda: (got(10),),
        2: lambda: (got(11), got_rest(10)),
        3: lambda: (from_mate(1),),
        4: lambda: (got(12), got_rest(11)),
        5: lambda: (from_mate(0),),
        6: lambda: (got(13), got_rest(12)),
        8: lambda: (got(14), got_rest(13)),
        10: lambda: (got(15), got_rest(14)),
        12: lambda: (got_rest(15),),
    }

    def body(turn, carry):
        for when, event in events.items():
            pl.when(turn == when)(lambda event=event: (event(), None)[1])
        work(pick(turn, [u for u, _ in ORDER]), pick(turn, [step for _, step in ORDER]))
        return carry

    lax.fori_loop(0, len(ORDER), body, 0)

    for u in (9, 8, 7, 6):
        to_outer(u).wait_send()
        to_mate(u).wait_send()
    for u in (6, 7):
        to_behind(u).wait_send()
    for u in range(10, 16):
        mine_to_peer(u).wait_send()
        if u < 12:
            mine_to_mate(u).wait_send()
            theirs_to_mate(u).wait_send()


def shards(hamiltonian, columns, sample):
    rows, slots, tile, _ = hamiltonian.shape
    devices = lax.axis_size("grid")
    assert rows == ROWS and devices >= 6
    dma = pltpu.SemaphoreType.DMA
    return pl.pallas_call(
        functools.partial(kernel, devices),
        out_shape=jax.ShapeDtypeStruct(hamiltonian.shape, jnp.float32),
        in_specs=[
            pl.BlockSpec(memory_space=pl.ANY),
            pl.BlockSpec(memory_space=pltpu.VMEM),
            pl.BlockSpec(memory_space=pltpu.SMEM),
        ],
        out_specs=pl.BlockSpec(memory_space=pltpu.VMEM),
        scratch_shapes=[
            pltpu.VMEM((SPAN, slots, tile, tile), jnp.float32),
            pltpu.VMEM((5, 8, 128), jnp.int32),
            pltpu.SMEM((5, 8, 128), jnp.int32),
            pltpu.VMEM((STEPS, SPAN * slots + 1, tile, tile), jnp.bfloat16),
            pltpu.VMEM((STEPS, SPAN * slots + 1, tile, tile), jnp.bfloat16),
            pltpu.VMEM((tile, tile), jnp.float32),
            pltpu.VMEM((slots * tile, slots * tile), jnp.bfloat16),
            pltpu.VMEM((slots * tile, slots * tile), jnp.bfloat16),
            pltpu.VMEM((2 * tile, slots * tile), jnp.bfloat16),
            pltpu.VMEM((2 * tile, slots * tile), jnp.bfloat16),
            dma((SPAN, 2)),
            dma((20,)),
            dma((5,)),
            dma((4,)),
            dma((4,)),
            dma,
        ],
        compiler_params=pltpu.CompilerParams(
            collective_id=0, has_side_effects=True, vmem_limit_bytes=40 * 2**20
        ),
    )(hamiltonian, columns, sample)


def solution(mesh):
    return jax.shard_map(
        shards,
        mesh=mesh,
        in_specs=(P("grid", None, None, None), P("grid", None), P("samples")),
        out_specs=P(("samples", "grid"), None, None, None),
        check_vma=False,
    )
```

```python
import functools

import jax
import jax.numpy as jnp
from jax import lax
from jax.experimental import pallas as pl
from jax.experimental.pallas import tpu as pltpu
from jax.sharding import PartitionSpec as P

REACH = 3
STEPS = 2
ROWS = 4
HALO = STEPS * REACH
SPAN = ROWS + 2 * HALO
MESH = pl.DeviceIdType.MESH

ORDER = ((5, 0), (6, 0), (7, 0), (4, 0), (8, 0), (3, 0), (9, 0), (6, 1), (10, 0), (7, 1), (11, 0), (8, 1), (12, 0), (9, 1))


def pick(index, values):
    chosen = jnp.int32(values[0])
    for at, value in enumerate(values[1:], 1):
        chosen = jnp.where(index == at, jnp.int32(value), chosen)
    return chosen


def kernel(
    devices, ham, columns, sample, out, ext, cbuf, csm, high, low, eye, ahigh, alow, left, left2,
    recv, send, crecv, csend, local, csem,
):
    me, s = lax.axis_index("grid"), lax.axis_index("samples")
    slots, tile = ham.shape[1], ham.shape[2]
    pair = slots // 2
    total = devices * ROWS
    zero_tile = SPAN * slots
    odd = lax.rem(me, 2)
    sign = 2 * odd - 1

    def at(offset):
        return (s, lax.rem(me + offset + devices, devices))

    mate, outer, behind, beyond = at(-sign), at(sign), at(-2 * sign), at(2 * sign)
    peer = (1 - s, me)

    def own(u):
        return jnp.where(odd == 1, u - HALO, HALO + ROWS - 1 - u)

    def mine(u):
        return ext.at[u, pl.ds(pair * s, pair)]

    def theirs(u):
        return ext.at[u, pl.ds(pair * (1 - s), pair)]

    def copy(source, target, send_sem, recv_sem, device):
        return pltpu.make_async_remote_copy(
            src_ref=source, dst_ref=target, send_sem=send_sem, recv_sem=recv_sem, device_id=device, device_id_type=MESH
        )

    def to_mate(u):
        return copy(ham.at[own(u)], ext.at[11 - u], send.at[u - 6], recv.at[11 - u, 0], mate)

    def to_outer(u):
        return copy(ham.at[own(u), pl.ds(pair * s, pair)], mine(19 - u), send.at[4 + u - 6], recv.at[19 - u, s], outer)

    def to_behind(u):
        return copy(ham.at[own(u), pl.ds(pair * s, pair)], mine(u + 8), send.at[8 + u - 6], recv.at[u + 8, s], behind)

    def last_to_behind():
        return copy(ham.at[own(7)], ext.at[15], send.at[9], recv.at[15, 0], behind)

    def mine_to_peer(u):
        return copy(mine(u), mine(u), send.at[10 + u - 10], recv.at[u, s], peer)

    def mine_to_mate(u):
        return copy(mine(u), mine(11 - u), send.at[16 + u - 10], recv.at[11 - u, s], mate)

    def theirs_to_mate(u):
        return copy(theirs(u), theirs(11 - u), send.at[18 + u - 10], recv.at[11 - u, 1 - s], mate)

    def theirs_from_peer(u):
        return copy(theirs(u), theirs(u), send.at[10 + u - 10], recv.at[u, 1 - s], peer)

    def keep(u):
        return pltpu.make_async_copy(ham.at[own(u)], ext.at[u], local.at[u - 6])

    def columns_to(index):
        slot, device = ((1, mate), (3, outer), (4, behind), (0, beyond))[index]
        return copy(cbuf.at[2], cbuf.at[slot], csend.at[index], crecv.at[slot], device)

    barrier = pltpu.get_barrier_semaphore()
    for device in (mate, outer, behind, beyond, peer):
        pl.semaphore_signal(barrier, inc=1, device_id=device, device_id_type=MESH)
    for u in range(6, 10):
        keep(u).start()
    cbuf[2, 0:ROWS, 0:slots] = columns[...]
    pl.semaphore_wait(barrier, 5)

    for index in range(4):
        columns_to(index).start()
    for u in (9, 8):
        to_outer(u).start()
    for u in (6, 7, 8, 9):
        to_mate(u).start()

    same = lax.broadcasted_iota(jnp.int32, (tile, tile), 0) == lax.broadcasted_iota(jnp.int32, (tile, tile), 1)
    eye[...] = same.astype(jnp.float32)
    for step in range(STEPS):
        high[step, zero_tile] = jnp.zeros((tile, tile), jnp.bfloat16)
        low[step, zero_tile] = jnp.zeros((tile, tile), jnp.bfloat16)
    radical = jnp.float32(0.0)
    for bit in range(10):
        radical += (lax.shift_right_logical(sample[0], bit) & 1).astype(jnp.float32) * jnp.float32(0.5 ** (bit + 1))
    chemical = -0.2 + 0.4 * radical

    for index in range(4):
        columns_to(index).wait()
    table = pltpu.make_async_copy(cbuf, csm, csem)
    table.start()
    table.wait()

    def column(u, slot):
        place = (u + 2) & 3
        return csm[lax.shift_right_logical(u + 2, 2), jnp.where(odd == 1, place, 3 - place), slot]

    def row_of(col):
        up = jnp.clip(lax.rem(col - ROWS * me + HALO + total, total), 0, SPAN - 1)
        return jnp.where(odd == 1, up, SPAN - 1 - up)

    def split(value):
        upper = value.astype(jnp.bfloat16)
        return upper, (value - upper.astype(jnp.float32)).astype(jnp.bfloat16)

    def begin(u):
        for m in range(slots):
            diagonal = eye[...] * jnp.where(row_of(column(u, m)) == u, 1.0, 0.0)
            tiles = 0.4 * (chemical * diagonal - ext[u, m]) + 0.5 * diagonal
            upper, lower = split(tiles)
            high[0, u * slots + m] = upper
            low[0, u * slots + m] = lower

    def begin_each(first, last):
        def body(u, carry):
            begin(u)
            return carry

        lax.fori_loop(first, last, body, 0)

    def got(u):
        mine_to_peer(u).wait_recv()
        mine_to_peer(u).start()
        if u < 12:
            mine_to_mate(u).start()
            to_outer(17 - u).start()
        elif u == 12:
            to_behind(6).start()
        elif u == 13:
            last_to_behind().start()

    def got_rest(u):
        theirs_from_peer(u).wait_recv()
        if u < 12:
            theirs_to_mate(u).start()
        begin(u)

    def from_mate(u):
        mine_to_mate(11 - u).wait_recv()
        theirs_to_mate(11 - u).wait_recv()
        begin(u)

    def times(lefts):
        both = jnp.dot(lefts[...], ahigh[...], preferred_element_type=jnp.float32)
        rest = jnp.dot(lefts[0:tile], alow[...], preferred_element_type=jnp.float32)
        return both[0:tile] + (both[tile:] + rest)

    def work(u, step):
        own_columns = [column(u, b) for b in range(slots)]
        for a in range(slots):
            row = row_of(own_columns[a])
            held = [column(row, m) for m in range(slots)]
            for b in range(slots):
                index = jnp.int32(zero_tile)
                for m in range(slots):
                    index = jnp.where(held[m] == own_columns[b], row * slots + m, index)
                ahigh[a * tile : (a + 1) * tile, b * tile : (b + 1) * tile] = high[step, index]
                alow[a * tile : (a + 1) * tile, b * tile : (b + 1) * tile] = low[step, index]
        for m in range(slots):
            left[0:tile, m * tile : (m + 1) * tile] = high[step, u * slots + m]
            left[tile:, m * tile : (m + 1) * tile] = low[step, u * slots + m]
        square = times(left)
        upper, lower = split(square)
        left2[0:tile] = upper
        left2[tile:] = lower
        density = 3.0 * square - 2.0 * times(left2)

        @pl.when(step == 0)
        def _():
            upper, lower = split(density)
            for b in range(slots):
                high[1, u * slots + b] = upper[:, b * tile : (b + 1) * tile]
                low[1, u * slots + b] = lower[:, b * tile : (b + 1) * tile]

        @pl.when(step == 1)
        def _():
            for b in range(slots):
                out[own(u), b] = density[:, b * tile : (b + 1) * tile]

    for u in range(6, 10):
        keep(u).wait()
    for u in range(6, 10):
        to_mate(u).wait_recv()
    begin_each(2, 10)

    events = {
        0: lambda: (got(10),),
        1: lambda: (got(11),),
        2: lambda: (got_rest(10),),
        3: lambda: (got(12), from_mate(1)),
        4: lambda: (got_rest(11),),
        5: lambda: (from_mate(0), got(13)),
        6: lambda: (got_rest(12),),
        7: lambda: (got(14),),
        8: lambda: (got_rest(13),),
        10: lambda: (got_rest(14),),
        12: lambda: (last_to_behind().wait_recv(), begin(15)),
    }

    def body(turn, carry):
        for when, event in events.items():
            pl.when(turn == when)(lambda event=event: (event(), None)[1])
        work(pick(turn, [u for u, _ in ORDER]), pick(turn, [step for _, step in ORDER]))
        return carry

    lax.fori_loop(0, len(ORDER), body, 0)

    for u in (9, 8, 7, 6):
        to_outer(u).wait_send()
        to_mate(u).wait_send()
    to_behind(6).wait_send()
    last_to_behind().wait_send()
    for u in range(10, 15):
        mine_to_peer(u).wait_send()
        if u < 12:
            mine_to_mate(u).wait_send()
            theirs_to_mate(u).wait_send()


def shards(hamiltonian, columns, sample):
    rows, slots, tile, _ = hamiltonian.shape
    devices = lax.axis_size("grid")
    assert rows == ROWS and devices >= 6
    dma = pltpu.SemaphoreType.DMA
    return pl.pallas_call(
        functools.partial(kernel, devices),
        out_shape=jax.ShapeDtypeStruct(hamiltonian.shape, jnp.float32),
        in_specs=[
            pl.BlockSpec(memory_space=pltpu.HBM),
            pl.BlockSpec(memory_space=pltpu.VMEM),
            pl.BlockSpec(memory_space=pltpu.SMEM),
        ],
        out_specs=pl.BlockSpec(memory_space=pltpu.VMEM),
        scratch_shapes=[
            pltpu.VMEM((SPAN, slots, tile, tile), jnp.float32),
            pltpu.VMEM((5, 8, 128), jnp.int32),
            pltpu.SMEM((5, 8, 128), jnp.int32),
            pltpu.VMEM((STEPS, SPAN * slots + 1, tile, tile), jnp.bfloat16),
            pltpu.VMEM((STEPS, SPAN * slots + 1, tile, tile), jnp.bfloat16),
            pltpu.VMEM((tile, tile), jnp.float32),
            pltpu.VMEM((slots * tile, slots * tile), jnp.bfloat16),
            pltpu.VMEM((slots * tile, slots * tile), jnp.bfloat16),
            pltpu.VMEM((2 * tile, slots * tile), jnp.bfloat16),
            pltpu.VMEM((2 * tile, slots * tile), jnp.bfloat16),
            dma((SPAN, 2)),
            dma((20,)),
            dma((5,)),
            dma((4,)),
            dma((4,)),
            dma,
        ],
        compiler_params=pltpu.CompilerParams(
            collective_id=0, has_side_effects=True, vmem_limit_bytes=40 * 2**20
        ),
    )(hamiltonian, columns, sample)


def solution(mesh):
    return jax.shard_map(
        shards,
        mesh=mesh,
        in_specs=(P("grid", None, None, None), P("grid", None), P("samples")),
        out_specs=P(("samples", "grid"), None, None, None),
        check_vma=False,
    )
```
